32 devices in a mesh: stream: 8 (over z, x), span: 4 (over y, core).
Axes of the slice: x: 2, y: 2, z: 4, core: 2. Of those that a mesh axis runs over, the one named last changes fastest.
Arguments:
- positions: float32 [64, 16, 3, 128], P('stream', 'span'), as said below
- velocities: float32 [64, 16, 3, 128], P('stream', 'span'), may hold values from -3 to 3
- strength: float32 [64, 16, 128], P('stream', 'span'), may hold values from 0.5 to 2
- noise: float32 [64, 16, 4, 128], P('stream', 'span'), may hold values from -4 to 4
- counts: int32 [64, 16], P('stream', 'span'), may hold values from 32 to 128
- wall_beads: float32 [64, 16, 3, 128], P('stream', 'span'), as said below
- wall_strength: float32 [64, 16, 128], P('stream', 'span'), may hold values from 0.5 to 2
- wall_faces: int32 [64, 16], P('stream', 'span'), may hold values from 0 to 8
Outputs:
- final_positions: float32 [64, 16, 3, 128], P('stream', 'span')
- final_velocities: float32 [64, 16, 3, 128], P('stream', 'span')
The draws below stay inside these ranges and needn't reach their ends.
Inputs may be any that keep to these rules, and one draw needn't show every extreme that they name: `positions`: bead i of every cell lies within 0.3 in x and y and within 0.06 in z of the point ((i mod 2) + 0.5, (floor(i / 2) mod 2) + 0.5, (floor(i / 4) + 0.5) / 3). `wall_beads`: wall bead offsets lie in [0, 2) in x and y and in [0, 32/3) in z.
All inputs are finite; a program needn't handle non-finite values.
Results may differ from the reference program's by a relative error of at most 0.0003.
Values sent between devices are 32-bit elements; how exact they have to be, the bound alone decides.
A program may use at most 64 MiB of HBM per device.

```python
import math
import jax
import jax.numpy as jnp
from jax import lax

BEADS = 128
STEPS = 3
RANDS = 4
GX = 64
GY = 16


def draw_positions(key, part):
    key = jax.random.fold_in(key, 11)
    slots = jnp.arange(128, dtype=jnp.int32)
    base_x = (slots % 2).astype(jnp.float32) + 0.5
    base_y = (slots // 2 % 2).astype(jnp.float32) + 0.5
    base_z = ((slots // 4).astype(jnp.float32) + 0.5) * (1.0 / 3.0)
    base = jnp.stack([base_x, base_y, base_z])
    jitter = jnp.clip(jax.random.normal(key, (GX, GY, 3, 128), jnp.float32), -2.0, 2.0)
    spread_rows = jnp.array([0.15, 0.15, 0.03], jnp.float32)
    return base + jitter * spread_rows[:, None]


def draw_wall_beads(key, part):
    key = jax.random.fold_in(key, 29)
    unit = jax.random.uniform(key, (GX, GY, 3, 128), jnp.float32, 0.0, 1.0)
    extent = jnp.array([2.0, 2.0, 32.0 / 3.0], jnp.float32)
    return unit * extent[:, None]


def with_ends(result, key, smallest, high):
    index_at = [jax.random.randint(jax.random.fold_in(key, axis), (), 0, length) for axis, length in enumerate(result.shape)]
    longest = result.shape.index(max(result.shape))
    beside = index_at[:longest] + [(index_at[longest] + 1) % result.shape[longest]] + index_at[longest + 1:]
    return result.at[tuple(index_at)].set(smallest).at[tuple(beside)].set(high)


def steps_of(rng, dims, shards, smallest, high):
    def one(axis_at, parts):
        draws = jax.random.uniform(jax.random.fold_in(jax.random.fold_in(rng, 6), axis_at), (parts,), jnp.float32, smallest / len(shards), high / len(shards))
        return jnp.repeat(jnp.exp(draws), dims[axis_at] // parts).reshape((-1,) + (1,) * (len(dims) - axis_at - 1))

    factor_of = one(*shards[0])
    for cut in shards[1:]:
        factor_of = factor_of * one(*cut)
    return factor_of


def gaussian(key, shape, scale, limit, split=(), kind=jnp.bfloat16):
    loudness = steps_of(key, shape, split, -0.22, 0.18) if split else 1.0
    entries = jax.random.normal(key, shape, jnp.float32) * scale * loudness
    return jnp.minimum(jnp.maximum(entries, -limit), limit).astype(kind)


def setup_inputs(seed: int = 0) -> dict:
    splits = jax.random.split(jax.random.key(seed), 9)
    return {
        "positions": draw_positions(jax.random.fold_in(splits[8], 71), 0),
        "velocities": gaussian(splits[1], (GX, GY, 3, BEADS), 1.0, 3.0, ((0, 8), (1, 4)), jnp.float32),
        "strength": jnp.clip(jnp.exp(math.log(2.0) - 1.3862944 * jax.random.uniform(splits[2], (GX, GY, BEADS), jnp.float32) ** steps_of(splits[2], (GX, GY, BEADS), ((0, 8), (1, 4)), -0.2, 0.2)), 0.5, 2.0),
        "noise": gaussian(splits[3], (GX, GY, RANDS, BEADS), 1.0, 4.0, ((0, 8), (1, 4)), jnp.float32),
        "counts": with_ends(jax.random.randint(splits[4], (GX, GY), 32, 129), jax.random.fold_in(splits[4], 1), 32, 128).astype(jnp.int32),
        "wall_beads": draw_wall_beads(jax.random.fold_in(splits[8], 71), 0),
        "wall_strength": jnp.clip(jnp.exp(math.log(2.0) - 1.3862944 * jax.random.uniform(splits[6], (GX, GY, BEADS), jnp.float32) ** steps_of(splits[6], (GX, GY, BEADS), ((0, 8), (1, 4)), -0.2, 0.2)), 0.5, 2.0),
        "wall_faces": with_ends(jax.random.randint(splits[7], (GX, GY), 0, 9), jax.random.fold_in(splits[7], 1), 0, 8).astype(jnp.int32),
    }


height = 32.0 / 3.0
cell_side = 2.0
soften = 0.01
repulse = 25.0
friction = 4.5
kick = 3.0
time_step = 0.01

def tile_force(own_cells, near_cells, shift_x, shift_y):
    delta_x = own_cells[:, 0, :, None] - (near_cells[:, 0, None, :] + shift_x)
    delta_y = own_cells[:, 1, :, None] - (near_cells[:, 1, None, :] + shift_y)
    delta_z = own_cells[:, 2, :, None] - near_cells[:, 2, None, :]
    delta_z = delta_z - height * jnp.floor(delta_z / height + 0.5)
    dist = jnp.sqrt(delta_x * delta_x + delta_y * delta_y + delta_z * delta_z + soften)
    weight = jnp.maximum(1.0 - dist, 0.0)
    rel_x = own_cells[:, 3, :, None] - near_cells[:, 3, None, :]
    rel_y = own_cells[:, 4, :, None] - near_cells[:, 4, None, :]
    rel_z = own_cells[:, 5, :, None] - near_cells[:, 5, None, :]
    project = (delta_x * rel_x + delta_y * rel_y + delta_z * rel_z) / dist
    alive = own_cells[:, 8, :, None] * near_cells[:, 8, None, :]
    repel = repulse * jnp.sqrt(own_cells[:, 6, :, None] * near_cells[:, 6, None, :])
    theta = (own_cells[:, 7, :, None] + near_cells[:, 7, None, :]) * math.sqrt(0.5)
    coeff = alive * weight * (repel - friction * weight * project + kick * theta / math.sqrt(time_step)) / dist
    return jnp.stack([lax.optimization_barrier(jnp.sum(coeff * delta_x, axis=-1)), lax.optimization_barrier(jnp.sum(coeff * delta_y, axis=-1)), lax.optimization_barrier(jnp.sum(coeff * delta_z, axis=-1))], axis=1)

def wall_force(own_cells, wall_cells, facing):
    delta_x = own_cells[:, 0, :, None] - wall_cells[:, 0, None, :]
    delta_y = own_cells[:, 1, :, None] - wall_cells[:, 1, None, :]
    delta_z = own_cells[:, 2, :, None] - wall_cells[:, 2, None, :]
    delta_z = delta_z - height * jnp.floor(delta_z / height + 0.5)
    dist = jnp.sqrt(delta_x * delta_x + delta_y * delta_y + delta_z * delta_z + soften)
    weight = jnp.maximum(1.0 - dist, 0.0)
    project = (delta_x * own_cells[:, 3, :, None] + delta_y * own_cells[:, 4, :, None] + delta_z * own_cells[:, 5, :, None]) / dist
    repel = repulse * jnp.sqrt(own_cells[:, 6, :, None] * wall_cells[:, 3, None, :])
    coeff = facing[:, None, None] * own_cells[:, 8, :, None] * weight * (repel - friction * weight * project) / dist
    return jnp.stack([lax.optimization_barrier(jnp.sum(coeff * delta_x, axis=-1)), lax.optimization_barrier(jnp.sum(coeff * delta_y, axis=-1)), lax.optimization_barrier(jnp.sum(coeff * delta_z, axis=-1))], axis=1)

def reference(positions, velocities, strength, noise, counts, wall_beads, wall_strength, wall_faces):
    slots = jnp.arange(positions.shape[-1], dtype=jnp.int32)
    live = (slots[None, None, :] < counts[:, :, None]).astype(positions.dtype)
    face_row = jnp.broadcast_to(wall_faces.astype(positions.dtype)[:, :, None, None], (GX, GY, 1, positions.shape[-1]))
    walls = jnp.concatenate([wall_beads, wall_strength[:, :, None, :], face_row], axis=2)
    wall_padded = jnp.pad(walls, ((1, 1), (1, 1), (0, 0), (0, 0)), mode='wrap')

    def forces(place, speed, noise_row):
        packed = jnp.concatenate([place, speed, strength[:, :, None, :], noise_row[:, :, None, :], live[:, :, None, :]], axis=2)
        padded = jnp.pad(packed, ((1, 1), (1, 1), (0, 0), (0, 0)), mode='wrap')

        def one_row(row_index):
            own_cells = lax.dynamic_index_in_dim(packed, row_index, 0, keepdims=False)
            total = jnp.zeros((GY, 3, own_cells.shape[-1]), place.dtype)
            for across in (-1, 0, 1):
                band = lax.dynamic_index_in_dim(padded, row_index + 1 + across, 0, keepdims=False)
                wall_band = lax.dynamic_index_in_dim(wall_padded, row_index + 1 + across, 0, keepdims=False)
                for along in (-1, 0, 1):
                    near_cells = band[1 + along:1 + along + GY]
                    total = total + tile_force(own_cells, near_cells, across * cell_side, along * cell_side)
                    near_walls = wall_band[1 + along:1 + along + GY]
                    wanted = float((1 - across) * 3 + (1 - along))
                    facing = (near_walls[:, 4, 0] == wanted).astype(place.dtype)
                    total = total + wall_force(own_cells, near_walls, facing)
            return total
        return lax.map(one_row, jnp.arange(GX, dtype=jnp.int32))
    place, speed = (positions, velocities)
    force = forces(place, speed, noise[:, :, 0, :])
    for step in range(STEPS):
        half = speed + 0.5 * time_step * force
        place = place + time_step * half
        force = forces(place, half, noise[:, :, step + 1, :])
        speed = half + 0.5 * time_step * force
    return (place, speed)
```

```python
import math

import jax
import jax.numpy as jnp
from jax import lax
from jax.experimental import pallas as pl
from jax.experimental.pallas import tpu as pltpu
from jax.sharding import PartitionSpec as P

STEPS = 3


height = 32.0 / 3.0
cell_side = 2.0
soften = 0.01
repulse = 25.0
friction = 4.5
kick = 3.0
time_step = 0.01


def padded_2(cells, sides, width):
    for axis, dim in sides:
        count = lax.axis_size(axis)
        head = lax.slice_in_dim(cells, 0, width, axis=dim)
        tail = lax.slice_in_dim(cells, cells.shape[dim] - width, cells.shape[dim], axis=dim)
        cells = jnp.concatenate(
            [
                lax.ppermute(tail, axis, [(i, (i + 1) % count) for i in range(count)]),
                cells,
                lax.ppermute(head, axis, [((i + 1) % count, i) for i in range(count)]),
            ],
            axis=dim,
        )
    return cells


def tile_force(own_cells, near_cells, shift_x, shift_y):
    delta_x = own_cells[:, 0, :, None] - (near_cells[:, 0, None, :] + shift_x)
    delta_y = own_cells[:, 1, :, None] - (near_cells[:, 1, None, :] + shift_y)
    delta_z = own_cells[:, 2, :, None] - near_cells[:, 2, None, :]
    delta_z = delta_z - height * jnp.floor(delta_z / height + 0.5)
    dist = jnp.sqrt(delta_x * delta_x + delta_y * delta_y + delta_z * delta_z + soften)
    weight = jnp.maximum(1.0 - dist, 0.0)
    rel_x = own_cells[:, 3, :, None] - near_cells[:, 3, None, :]
    rel_y = own_cells[:, 4, :, None] - near_cells[:, 4, None, :]
    rel_z = own_cells[:, 5, :, None] - near_cells[:, 5, None, :]
    project = (delta_x * rel_x + delta_y * rel_y + delta_z * rel_z) / dist
    alive = own_cells[:, 8, :, None] * near_cells[:, 8, None, :]
    repel = repulse * jnp.sqrt(own_cells[:, 6, :, None] * near_cells[:, 6, None, :])
    theta = (own_cells[:, 7, :, None] + near_cells[:, 7, None, :]) * math.sqrt(0.5)
    coeff = (
        alive
        * weight
        * (repel - friction * weight * project + kick * theta / math.sqrt(time_step))
        / dist
    )
    return jnp.stack(
        [
            jnp.sum(coeff * delta_x, axis=-1),
            jnp.sum(coeff * delta_y, axis=-1),
            jnp.sum(coeff * delta_z, axis=-1),
        ],
        axis=1,
    )


def wall_force(own_cells, wall_cells, facing):
    delta_x = own_cells[:, 0, :, None] - wall_cells[:, 0, None, :]
    delta_y = own_cells[:, 1, :, None] - wall_cells[:, 1, None, :]
    delta_z = own_cells[:, 2, :, None] - wall_cells[:, 2, None, :]
    delta_z = delta_z - height * jnp.floor(delta_z / height + 0.5)
    dist = jnp.sqrt(delta_x * delta_x + delta_y * delta_y + delta_z * delta_z + soften)
    weight = jnp.maximum(1.0 - dist, 0.0)
    project = (
        delta_x * own_cells[:, 3, :, None]
        + delta_y * own_cells[:, 4, :, None]
        + delta_z * own_cells[:, 5, :, None]
    ) / dist
    repel = repulse * jnp.sqrt(own_cells[:, 6, :, None] * wall_cells[:, 3, None, :])
    coeff = (
        facing[:, None, None]
        * own_cells[:, 8, :, None]
        * weight
        * (repel - friction * weight * project)
        / dist
    )
    return jnp.stack(
        [
            jnp.sum(coeff * delta_x, axis=-1),
            jnp.sum(coeff * delta_y, axis=-1),
            jnp.sum(coeff * delta_z, axis=-1),
        ],
        axis=1,
    )


def extend(packed):
    return padded_2(packed, (("stream", 0), ("span", 1)), 1)


def forces(place, speed, strength, noise_row, live, wall_padded):
    packed = jnp.concatenate(
        [place, speed, strength[:, :, None, :], noise_row[:, :, None, :], live[:, :, None, :]],
        axis=2,
    )
    padded = extend(packed)
    rows_here = packed.shape[0]
    cols_here = packed.shape[1]
    slots = packed.shape[-1]
    own_cells = packed.reshape(rows_here * cols_here, 9, slots)
    total = jnp.zeros((rows_here * cols_here, 3, slots), place.dtype)
    for across in (-1, 0, 1):
        for along in (-1, 0, 1):
            near_cells = padded[
                1 + across : 1 + across + rows_here, 1 + along : 1 + along + cols_here
            ]
            near_cells = near_cells.reshape(rows_here * cols_here, 9, slots)
            total = total + tile_force(own_cells, near_cells, across * cell_side, along * cell_side)
            near_walls = wall_padded[
                1 + across : 1 + across + rows_here, 1 + along : 1 + along + cols_here
            ]
            near_walls = near_walls.reshape(rows_here * cols_here, 5, slots)
            wanted = float((1 - across) * 3 + (1 - along))
            facing = (near_walls[:, 4, 0] == wanted).astype(place.dtype)
            total = total + wall_force(own_cells, near_walls, facing)
    return total.reshape(rows_here, cols_here, 3, slots)


def every_pair(positions, velocities, strength, noise, counts, wall_beads, wall_strength, wall_faces):
    slots = jnp.arange(positions.shape[-1], dtype=jnp.int32)
    live = (slots[None, None, :] < counts[:, :, None]).astype(positions.dtype)
    face_row = jnp.broadcast_to(
        wall_faces.astype(positions.dtype)[:, :, None, None],
        (positions.shape[0], positions.shape[1], 1, positions.shape[-1]),
    )
    walls = jnp.concatenate([wall_beads, wall_strength[:, :, None, :], face_row], axis=2)
    wall_padded = padded_2(walls, (("stream", 0), ("span", 1)), 1)
    place, speed = (positions, velocities)
    force = forces(place, speed, strength, noise[:, :, 0, :], live, wall_padded)
    for step in range(STEPS):
        half = speed + 0.5 * time_step * force
        place = place + time_step * half
        force = forces(place, half, strength, noise[:, :, step + 1, :], live, wall_padded)
        speed = half + 0.5 * time_step * force
    return (place, speed)


REACH_XY = 0.49
REACH_Z = 0.33
FAR = 1.0e4
OWN = 8
STATIC = 10
MESH = pl.DeviceIdType.MESH


def lattice(shape):
    lane = lax.broadcasted_iota(jnp.int32, shape, len(shape) - 1)
    return lane, (
        (lane % 2).astype(jnp.float32) + 0.5,
        (lane // 2 % 2).astype(jnp.float32) + 0.5,
        ((lane // 4).astype(jnp.float32) + 0.5) * (1.0 / 3.0),
    )


def kernel(
    counts_ref, faces_ref, pos_ref, vel_ref, str_ref, noise_ref, wall_ref, wstr_ref,
    out_x, out_v, bad_ref,
    cells, own, now, live_ref, wide, target, push, near, force, send_sem, recv_sem,
):
    tx, ty = lax.axis_size("stream"), lax.axis_size("span")
    ix, iy = lax.axis_index("stream"), lax.axis_index("span")
    around = [(p, q) for p in (-1, 0, 1) for q in (-1, 0, 1) if (p, q) != (0, 0)]

    def device(p, q):
        return (lax.rem(ix + p + tx, tx), lax.rem(iy + q + ty, ty))

    barrier = pltpu.get_barrier_semaphore()
    for p, q in around:
        pl.semaphore_signal(barrier, inc=1, device_id=device(p, q), device_id_type=MESH)

    lane, point = lattice((8, 128))
    lane_row = lax.broadcasted_iota(jnp.int32, (1, 128), 1)

    for cx in range(8):
        for cy in range(4):
            row = pl.ds(OWN + cx, 1)
            live_ref[cy, pl.ds(cx, 1), :] = jnp.where(
                lane_row < counts_ref[cx, cy], 1.0, 0.0
            ).astype(jnp.float32)
            for c in range(3):
                now[c, cy, pl.ds(cx, 1), :] = pos_ref[cx, cy, pl.ds(c, 1), :]
                now[3 + c, cy, pl.ds(cx, 1), :] = vel_ref[cx, cy, pl.ds(c, 1), :]
                cells[5 + c, 1 + cy, row, :] = wall_ref[cx, cy, pl.ds(c, 1), :]
            for c in range(4):
                cells[1 + c, 1 + cy, row, :] = noise_ref[cx, cy, pl.ds(c, 1), :] * (
                    kick * math.sqrt(0.5) / math.sqrt(time_step)
                )
            cells[0, 1 + cy, row, :] = 5.0 * jnp.sqrt(str_ref[cx, pl.ds(cy, 1), :])
            cells[8, 1 + cy, row, :] = 5.0 * jnp.sqrt(wstr_ref[cx, pl.ds(cy, 1), :])
            cells[9, 1 + cy, row, :] = jnp.zeros((1, 128), jnp.float32) + faces_ref[cx, cy].astype(
                jnp.float32
            )
    own[...] = jnp.full(own.shape, FAR, jnp.float32)
    for cy in range(4):
        own[6, cy, pl.ds(OWN, 8), :] = cells[0, 1 + cy, pl.ds(OWN, 8), :]
    bad_ref[...] = jnp.zeros((8, 128), jnp.float32)

    def edge(p, q, first, count):
        rows = {-1: (OWN, OWN + 8, 1), 0: (OWN, OWN, 8), 1: (OWN + 7, OWN - 1, 1)}[p]
        cols = {-1: (1, 5, 1), 0: (1, 1, 4), 1: (4, 0, 1)}[q]
        comps = pl.ds(first, count)
        return (
            cells.at[comps, pl.ds(cols[0], cols[2]), pl.ds(rows[0], rows[2]), :],
            cells.at[comps, pl.ds(cols[1], cols[2]), pl.ds(rows[1], rows[2]), :],
        )

    def publish(t):
        first = STATIC + 6 * t
        bad = bad_ref[...]
        for cy in range(4):
            live = live_ref[cy] > 0.5
            for c in range(3):
                offset = now[c, cy] - point[c]
                limit = REACH_Z if c == 2 else REACH_XY
                fits = jnp.abs(offset) <= limit
                bad = jnp.maximum(bad, jnp.where(live, jnp.where(fits, 0.0, 1.0), 0.0))
                offset = jnp.where(live, offset, FAR)
                speed = friction * now[3 + c, cy]
                cells[first + c, 1 + cy, pl.ds(OWN, 8), :] = offset
                cells[first + 3 + c, 1 + cy, pl.ds(OWN, 8), :] = speed
                own[c, cy, pl.ds(OWN, 8), :] = offset
                own[3 + c, cy, pl.ds(OWN, 8), :] = speed
        bad_ref[...] = bad
        copies = []
        for n, (p, q) in enumerate(around):
            src, dst = edge(p, q, 0 if t == 0 else first, STATIC + 6 if t == 0 else 6)
            copy = pltpu.make_async_remote_copy(
                src_ref=src,
                dst_ref=dst,
                send_sem=send_sem.at[t, n],
                recv_sem=recv_sem.at[t, n],
                device_id=device(p, q),
                device_id_type=MESH,
            )
            copy.start()
            copies.append(copy)
        return copies

    def widen(cy, base, rows, block_of):
        tiles = [cells[5 + c, cy, pl.ds(base, 8), :].T for c in range(4)]
        for s in rows:
            block = block_of(s)
            for c in range(4):
                for part in range(16):
                    column = jnp.broadcast_to(tiles[c][8 * part : 8 * part + 8, s : s + 1], (8, 128))
                    if c < 3:
                        column = column - point[c]
                    if c == 2:
                        column = column - height * jnp.floor(column * (1.0 / height) + 0.5)
                    wide[block, c, pl.ds(8 * part, 8), :] = column

    def aim(cy, base, rows):
        face = cells[9, cy, pl.ds(base, 8), :]
        found = [jnp.full((8, 128), FAR, jnp.float32)] * 3 + [jnp.zeros((8, 128), jnp.float32)] * 4
        for q in (-1, 0, 1):
            if not 1 <= cy + q <= 4:
                continue
            for p in (-1, 0, 1):
                if (base < OWN and p != 1) or (base > OWN and p != -1):
                    continue
                hit = face == float(3 * (p + 1) + (q + 1))
                for c in range(7):
                    found[c] = jnp.where(
                        hit, own[c, cy + q - 1, pl.ds(base + p, 8), :], found[c]
                    )
        for c in range(7):
            target[c, cy, pl.ds(base, 8), :] = found[c]

    def aim_own():
        for cy in range(1, 5):
            aim(cy, OWN, None)

    def aim_ring():
        for cy in (0, 5):
            aim(cy, OWN, None)
        for cy in range(6):
            aim(cy, OWN - 8, None)
            aim(cy, OWN + 8, None)

    def wall_block(block, cy, row):
        at = [
            jnp.broadcast_to(target[c, cy, pl.ds(row, 1), :], (8, 128)) for c in range(7)
        ]
        total = [jnp.zeros((8, 128), jnp.float32) for _ in range(3)]
        for part in range(16):
            d = [at[c] - wide[block, c, pl.ds(8 * part, 8), :] for c in range(3)]
            square = d[0] * d[0] + d[1] * d[1] + (d[2] * d[2] + soften)
            inverse = lax.rsqrt(square)
            weight = jnp.maximum(1.0 - square * inverse, 0.0) * inverse
            dot = d[0] * at[3] + d[1] * at[4] + d[2] * at[5]
            repel = at[6] * wide[block, 3, pl.ds(8 * part, 8), :]
            coeff = weight * (repel - weight * dot)
            total = [total[c] + coeff * d[c] for c in range(3)]
        for c in range(3):
            push[c, cy, pl.ds(row, 1), :] = jnp.sum(total[c], axis=0, keepdims=True)

    def walls_rows(low, high):
        def body(b, carry):
            wall_block(b, b // 8, OWN + b % 8)
            return carry

        lax.fori_loop(low, high, body, 0)

    def walls_sides():
        def body(h, carry):
            wall_block(48 + h, h % 6, OWN - 1 + 9 * (h // 6))
            return carry

        lax.fori_loop(0, 12, body, 0)

    def swap(value, step, low):
        return jnp.where(low, pltpu.roll(value, 128 - step, 1), pltpu.roll(value, step, 1))

    low_x = lane % 2 == 0
    low_y = lane // 2 % 2 == 0

    def gather_near(t):
        def body(c, carry):
            comp = jnp.where(c < 6, STATIC + 6 * t + c, jnp.where(c == 6, 0, 1 + t))
            is_x = jnp.where(c == 0, 1.0, 0.0)
            is_y = jnp.where(c == 1, 1.0, 0.0)
            along_x = {-1: [], 0: [], 1: []}
            for cy in range(6):
                mid = cells[comp, cy, pl.ds(OWN, 8), :]
                before = cells[comp, cy, pl.ds(OWN - 1, 8), :]
                after = cells[comp, cy, pl.ds(OWN + 1, 8), :]
                along_x[0].append(mid)
                along_x[1].append(swap(jnp.where(low_x, after, mid), 1, low_x) + is_x)
                along_x[-1].append(swap(jnp.where(low_x, mid, before), 1, low_x) - is_x)
            for p in (-1, 0, 1):
                for cy in range(1, 5):
                    mid, before, after = (along_x[p][cy + q] for q in (0, -1, 1))
                    near[3 * (p + 1) + 1, c, cy - 1] = mid
                    near[3 * (p + 1) + 2, c, cy - 1] = (
                        swap(jnp.where(low_y, after, mid), 2, low_y) + is_y
                    )
                    near[3 * (p + 1), c, cy - 1] = (
                        swap(jnp.where(low_y, mid, before), 2, low_y) - is_y
                    )
            return carry

        lax.fori_loop(0, 8, body, 0)

    def pairs(cy, layer):
        shift = lax.rem(4 * layer + 128, 128)
        back = lax.rem(128 - 4 * layer, 128)
        me = [pltpu.roll(near[4, c, cy], shift, 1) for c in range(8)]
        me[2] = me[2] - layer.astype(jnp.float32) * (1.0 / 3.0)
        total = [jnp.zeros((8, 128), jnp.float32) for _ in range(3)]
        for side in range(9):
            other = [near[side, c, cy] for c in range(8)]
            d = [me[c] - other[c] for c in range(3)]
            square = d[0] * d[0] + d[1] * d[1] + (d[2] * d[2] + soften)
            inverse = lax.rsqrt(square)
            weight = jnp.maximum(1.0 - square * inverse, 0.0) * inverse
            dot = (
                d[0] * (me[3] - other[3]) + d[1] * (me[4] - other[4]) + d[2] * (me[5] - other[5])
            )
            base = me[6] * other[6] + (me[7] + other[7])
            coeff = weight * (base - weight * dot)
            total = [total[c] + coeff * d[c] for c in range(3)]
        return [pltpu.roll(total[c], back, 1) for c in range(3)]

    def all_pairs():
        def cell_body(cy, carry):
            def body(n, total):
                part = pairs(cy, n - 4)
                return tuple(total[c] + part[c] for c in range(3))

            zero = jnp.zeros((8, 128), jnp.float32)
            total = lax.fori_loop(0, 9, body, (zero, zero, zero))
            for c in range(3):
                force[c, cy] = total[c]
            return carry

        lax.fori_loop(0, 4, cell_body, 0)

    def collect():
        for cy in range(1, 5):
            total = [force[c, cy - 1] for c in range(3)]
            for p in (-1, 0, 1):
                for q in (-1, 0, 1):
                    rows = pl.ds(OWN - p, 8)
                    hit = cells[9, cy - q, rows, :] == float(3 * (p + 1) + (q + 1))
                    for c in range(3):
                        total[c] = total[c] + jnp.where(hit, push[c, cy - q, rows, :], 0.0)
            for c in range(3):
                force[c, cy - 1] = total[c] * live_ref[cy - 1]

    for t in range(STEPS + 1):
        if t > 0:
            for cy in range(4):
                for c in range(3):
                    half = now[3 + c, cy] + 0.5 * time_step * force[c, cy]
                    now[3 + c, cy] = half
                    now[c, cy] = now[c, cy] + time_step * half
        if t == 0:
            pl.semaphore_wait(barrier, 8)
        copies = publish(t)
        aim_own()
        if t == 0:
            for cy in range(1, 5):
                widen(cy, OWN, range(8), lambda s, cy=cy: 8 * cy + s)
            walls_rows(8, 40)
            for copy in copies:
                copy.wait_recv()
            for cy in (0, 5):
                widen(cy, OWN, range(8), lambda s, cy=cy: 8 * cy + s)
            for cy in range(6):
                widen(cy, OWN - 8, (7,), lambda s, cy=cy: 48 + cy)
                widen(cy, OWN + 8, (0,), lambda s, cy=cy: 54 + cy)
            aim_ring()
            walls_rows(0, 8)
            walls_rows(40, 48)
            walls_sides()
        else:
            aim_ring()
            walls_rows(0, 48)
            walls_sides()
            for copy in copies:
                copy.wait_recv()
        gather_near(t)
        all_pairs()
        collect()
        for copy in copies:
            copy.wait_send()
        if t > 0:
            for cy in range(4):
                for c in range(3):
                    now[3 + c, cy] = now[3 + c, cy] + 0.5 * time_step * force[c, cy]

    for cx in range(8):
        for cy in range(4):
            for c in range(3):
                out_x[cx, cy, pl.ds(c, 1), :] = now[c, cy, pl.ds(cx, 1), :]
                out_v[cx, cy, pl.ds(c, 1), :] = now[3 + c, cy, pl.ds(cx, 1), :]


def near_only(positions, velocities, strength, noise, counts, wall_beads, wall_strength, wall_faces):
    vmem = pl.BlockSpec(memory_space=pltpu.VMEM)
    smem = pl.BlockSpec(memory_space=pltpu.SMEM)
    f32 = jnp.float32
    return pl.pallas_call(
        kernel,
        out_shape=(
            jax.ShapeDtypeStruct(positions.shape, f32),
            jax.ShapeDtypeStruct(velocities.shape, f32),
            jax.ShapeDtypeStruct((8, 128), f32),
        ),
        in_specs=[smem, smem] + [vmem] * 6,
        out_specs=(vmem, vmem, vmem),
        scratch_shapes=[
            pltpu.VMEM((STATIC + 6 * (STEPS + 1), 6, 24, 128), f32),
            pltpu.VMEM((7, 4, 32, 128), f32),
            pltpu.VMEM((6, 4, 8, 128), f32),
            pltpu.VMEM((4, 8, 128), f32),
            pltpu.VMEM((60, 4, 128, 128), f32),
            pltpu.VMEM((7, 6, 24, 128), f32),
            pltpu.VMEM((3, 6, 24, 128), f32),
            pltpu.VMEM((9, 8, 4, 8, 128), f32),
            pltpu.VMEM((3, 4, 8, 128), f32),
            pltpu.SemaphoreType.DMA((STEPS + 1, 8)),
            pltpu.SemaphoreType.DMA((STEPS + 1, 8)),
        ],
        compiler_params=pltpu.CompilerParams(
            collective_id=0, has_side_effects=True, vmem_limit_bytes=48 * 2**20
        ),
    )(counts, wall_faces, positions, velocities, strength, noise, wall_beads, wall_strength)


def local(*args):
    x, v, bad = near_only(*args)
    worst = lax.pmax(jnp.max(bad), ("stream", "span"))
    return lax.cond(worst > 0.0, lambda: every_pair(*args), lambda: (x, v))


def solution(mesh):
    in_specs = (
        P("stream", "span", None, None),
        P("stream", "span", None, None),
        P("stream", "span", None),
        P("stream", "span", None, None),
        P("stream", "span"),
        P("stream", "span", None, None),
        P("stream", "span", None),
        P("stream", "span"),
    )
    out_specs = (P("stream", "span", None, None), P("stream", "span", None, None))
    return jax.shard_map(local, mesh=mesh, in_specs=in_specs, out_specs=out_specs, check_vma=False)
```

```python
import math

import jax
import jax.numpy as jnp
from jax import lax
from jax.experimental import pallas as pl
from jax.experimental.pallas import tpu as pltpu
from jax.sharding import PartitionSpec as P

STEPS = 3


height = 32.0 / 3.0
cell_side = 2.0
soften = 0.01
repulse = 25.0
friction = 4.5
kick = 3.0
time_step = 0.01


def padded_2(cells, sides, width):
    for axis, dim in sides:
        count = lax.axis_size(axis)
        head = lax.slice_in_dim(cells, 0, width, axis=dim)
        tail = lax.slice_in_dim(cells, cells.shape[dim] - width, cells.shape[dim], axis=dim)
        cells = jnp.concatenate(
            [
                lax.ppermute(tail, axis, [(i, (i + 1) % count) for i in range(count)]),
                cells,
                lax.ppermute(head, axis, [((i + 1) % count, i) for i in range(count)]),
            ],
            axis=dim,
        )
    return cells


def tile_force(own_cells, near_cells, shift_x, shift_y):
    delta_x = own_cells[:, 0, :, None] - (near_cells[:, 0, None, :] + shift_x)
    delta_y = own_cells[:, 1, :, None] - (near_cells[:, 1, None, :] + shift_y)
    delta_z = own_cells[:, 2, :, None] - near_cells[:, 2, None, :]
    delta_z = delta_z - height * jnp.floor(delta_z / height + 0.5)
    dist = jnp.sqrt(delta_x * delta_x + delta_y * delta_y + delta_z * delta_z + soften)
    weight = jnp.maximum(1.0 - dist, 0.0)
    rel_x = own_cells[:, 3, :, None] - near_cells[:, 3, None, :]
    rel_y = own_cells[:, 4, :, None] - near_cells[:, 4, None, :]
    rel_z = own_cells[:, 5, :, None] - near_cells[:, 5, None, :]
    project = (delta_x * rel_x + delta_y * rel_y + delta_z * rel_z) / dist
    alive = own_cells[:, 8, :, None] * near_cells[:, 8, None, :]
    repel = repulse * jnp.sqrt(own_cells[:, 6, :, None] * near_cells[:, 6, None, :])
    theta = (own_cells[:, 7, :, None] + near_cells[:, 7, None, :]) * math.sqrt(0.5)
    coeff = (
        alive
        * weight
        * (repel - friction * weight * project + kick * theta / math.sqrt(time_step))
        / dist
    )
    return jnp.stack(
        [
            jnp.sum(coeff * delta_x, axis=-1),
            jnp.sum(coeff * delta_y, axis=-1),
            jnp.sum(coeff * delta_z, axis=-1),
        ],
        axis=1,
    )


def wall_force(own_cells, wall_cells, facing):
    delta_x = own_cells[:, 0, :, None] - wall_cells[:, 0, None, :]
    delta_y = own_cells[:, 1, :, None] - wall_cells[:, 1, None, :]
    delta_z = own_cells[:, 2, :, None] - wall_cells[:, 2, None, :]
    delta_z = delta_z - height * jnp.floor(delta_z / height + 0.5)
    dist = jnp.sqrt(delta_x * delta_x + delta_y * delta_y + delta_z * delta_z + soften)
    weight = jnp.maximum(1.0 - dist, 0.0)
    project = (
        delta_x * own_cells[:, 3, :, None]
        + delta_y * own_cells[:, 4, :, None]
        + delta_z * own_cells[:, 5, :, None]
    ) / dist
    repel = repulse * jnp.sqrt(own_cells[:, 6, :, None] * wall_cells[:, 3, None, :])
    coeff = (
        facing[:, None, None]
        * own_cells[:, 8, :, None]
        * weight
        * (repel - friction * weight * project)
        / dist
    )
    return jnp.stack(
        [
            jnp.sum(coeff * delta_x, axis=-1),
            jnp.sum(coeff * delta_y, axis=-1),
            jnp.sum(coeff * delta_z, axis=-1),
        ],
        axis=1,
    )


def extend(packed):
    return padded_2(packed, (("stream", 0), ("span", 1)), 1)


def forces(place, speed, strength, noise_row, live, wall_padded):
    packed = jnp.concatenate(
        [place, speed, strength[:, :, None, :], noise_row[:, :, None, :], live[:, :, None, :]],
        axis=2,
    )
    padded = extend(packed)
    rows_here = packed.shape[0]
    cols_here = packed.shape[1]
    slots = packed.shape[-1]
    own_cells = packed.reshape(rows_here * cols_here, 9, slots)
    total = jnp.zeros((rows_here * cols_here, 3, slots), place.dtype)
    for across in (-1, 0, 1):
        for along in (-1, 0, 1):
            near_cells = padded[
                1 + across : 1 + across + rows_here, 1 + along : 1 + along + cols_here
            ]
            near_cells = near_cells.reshape(rows_here * cols_here, 9, slots)
            total = total + tile_force(own_cells, near_cells, across * cell_side, along * cell_side)
            near_walls = wall_padded[
                1 + across : 1 + across + rows_here, 1 + along : 1 + along + cols_here
            ]
            near_walls = near_walls.reshape(rows_here * cols_here, 5, slots)
            wanted = float((1 - across) * 3 + (1 - along))
            facing = (near_walls[:, 4, 0] == wanted).astype(place.dtype)
            total = total + wall_force(own_cells, near_walls, facing)
    return total.reshape(rows_here, cols_here, 3, slots)


def every_pair(positions, velocities, strength, noise, counts, wall_beads, wall_strength, wall_faces):
    slots = jnp.arange(positions.shape[-1], dtype=jnp.int32)
    live = (slots[None, None, :] < counts[:, :, None]).astype(positions.dtype)
    face_row = jnp.broadcast_to(
        wall_faces.astype(positions.dtype)[:, :, None, None],
        (positions.shape[0], positions.shape[1], 1, positions.shape[-1]),
    )
    walls = jnp.concatenate([wall_beads, wall_strength[:, :, None, :], face_row], axis=2)
    wall_padded = padded_2(walls, (("stream", 0), ("span", 1)), 1)
    place, speed = (positions, velocities)
    force = forces(place, speed, strength, noise[:, :, 0, :], live, wall_padded)
    for step in range(STEPS):
        half = speed + 0.5 * time_step * force
        place = place + time_step * half
        force = forces(place, half, strength, noise[:, :, step + 1, :], live, wall_padded)
        speed = half + 0.5 * time_step * force
    return (place, speed)


REACH_XY = 0.49
REACH_Z = 0.33
FAR = 1.0e4
OWN = 8
STATIC = 10
MESH = pl.DeviceIdType.MESH


def lattice(shape):
    lane = lax.broadcasted_iota(jnp.int32, shape, len(shape) - 1)
    return lane, (
        (lane % 2).astype(jnp.float32) + 0.5,
        (lane // 2 % 2).astype(jnp.float32) + 0.5,
        ((lane // 4).astype(jnp.float32) + 0.5) * (1.0 / 3.0),
    )


def kernel(
    counts_ref, faces_ref, pos_ref, vel_ref, str_ref, noise_ref, wall_ref, wstr_ref,
    out_x, out_v, bad_ref,
    cells, own, now, live_ref, wide, target, push, near, force, flags, send_sem, recv_sem, flag_send, flag_recv,
):
    tx, ty = lax.axis_size("stream"), lax.axis_size("span")
    ix, iy = lax.axis_index("stream"), lax.axis_index("span")
    around = [(p, q) for p in (-1, 0, 1) for q in (-1, 0, 1) if (p, q) != (0, 0)]

    def device(p, q):
        return (lax.rem(ix + p + tx, tx), lax.rem(iy + q + ty, ty))

    barrier = pltpu.get_barrier_semaphore()
    row_of = [(p, 0) for p in range(1, tx)]
    col_of = [(0, q) for q in range(1, ty)]
    greeted = row_of + col_of + [(p, q) for p, q in around if p * q != 0]
    for p, q in greeted:
        pl.semaphore_signal(barrier, inc=1, device_id=device(p, q), device_id_type=MESH)

    lane, point = lattice((8, 128))
    lane_row = lax.broadcasted_iota(jnp.int32, (1, 128), 1)

    for cx in range(8):
        for cy in range(4):
            row = pl.ds(OWN + cx, 1)
            live_ref[cy, pl.ds(cx, 1), :] = jnp.where(
                lane_row < counts_ref[cx, cy], 1.0, 0.0
            ).astype(jnp.float32)
            for c in range(3):
                now[c, cy, pl.ds(cx, 1), :] = pos_ref[cx, cy, pl.ds(c, 1), :]
                now[3 + c, cy, pl.ds(cx, 1), :] = vel_ref[cx, cy, pl.ds(c, 1), :]
                cells[5 + c, 1 + cy, row, :] = wall_ref[cx, cy, pl.ds(c, 1), :]
            for c in range(4):
                cells[1 + c, 1 + cy, row, :] = noise_ref[cx, cy, pl.ds(c, 1), :] * (
                    kick * math.sqrt(0.5) / math.sqrt(time_step)
                )
            cells[0, 1 + cy, row, :] = 5.0 * jnp.sqrt(str_ref[cx, pl.ds(cy, 1), :])
            cells[8, 1 + cy, row, :] = 5.0 * jnp.sqrt(wstr_ref[cx, pl.ds(cy, 1), :])
            cells[9, 1 + cy, row, :] = jnp.zeros((1, 128), jnp.float32) + faces_ref[cx, cy].astype(
                jnp.float32
            )
    own[...] = jnp.full(own.shape, FAR, jnp.float32)
    for cy in range(4):
        own[6, cy, pl.ds(OWN, 8), :] = cells[0, 1 + cy, pl.ds(OWN, 8), :]
    bad_ref[...] = jnp.zeros((8, 128), jnp.float32)

    def edge(p, q, first, count):
        rows = {-1: (OWN, OWN + 8, 1), 0: (OWN, OWN, 8), 1: (OWN + 7, OWN - 1, 1)}[p]
        cols = {-1: (1, 5, 1), 0: (1, 1, 4), 1: (4, 0, 1)}[q]
        comps = pl.ds(first, count)
        return (
            cells.at[comps, pl.ds(cols[0], cols[2]), pl.ds(rows[0], rows[2]), :],
            cells.at[comps, pl.ds(cols[1], cols[2]), pl.ds(rows[1], rows[2]), :],
        )

    def publish(t):
        first = STATIC + 6 * t
        bad = bad_ref[...]
        for cy in range(4):
            live = live_ref[cy] > 0.5
            for c in range(3):
                offset = now[c, cy] - point[c]
                limit = REACH_Z if c == 2 else REACH_XY
                fits = jnp.abs(offset) <= limit
                bad = jnp.maximum(bad, jnp.where(live, jnp.where(fits, 0.0, 1.0), 0.0))
                offset = jnp.where(live, offset, FAR)
                speed = friction * now[3 + c, cy]
                cells[first + c, 1 + cy, pl.ds(OWN, 8), :] = offset
                cells[first + 3 + c, 1 + cy, pl.ds(OWN, 8), :] = speed
                own[c, cy, pl.ds(OWN, 8), :] = offset
                own[3 + c, cy, pl.ds(OWN, 8), :] = speed
        bad_ref[...] = bad
        copies = []
        for n, (p, q) in enumerate(around):
            src, dst = edge(p, q, 0 if t == 0 else first, STATIC + 6 if t == 0 else 6)
            copy = pltpu.make_async_remote_copy(
                src_ref=src,
                dst_ref=dst,
                send_sem=send_sem.at[t, n],
                recv_sem=recv_sem.at[t, n],
                device_id=device(p, q),
                device_id_type=MESH,
            )
            copy.start()
            copies.append(copy)
        return copies

    def spread(source, first, offsets):
        sent = []
        for n, (p, q) in enumerate(offsets):
            copy = pltpu.make_async_remote_copy(
                src_ref=flags.at[source],
                dst_ref=flags.at[2 + first + n],
                send_sem=flag_send.at[first + n],
                recv_sem=flag_recv.at[first + n],
                device_id=device(p, q),
                device_id_type=MESH,
            )
            copy.start()
            sent.append(copy)
        return sent

    def merged(source, first, sent):
        worst = flags[source]
        for n, copy in enumerate(sent):
            copy.wait_recv()
            worst = jnp.maximum(worst, flags[2 + first + n])
        return worst

    def widen(cy, base, rows, block_of):
        tiles = [cells[5 + c, cy, pl.ds(base, 8), :].T for c in range(4)]
        for s in rows:
            block = block_of(s)
            for c in range(4):
                for part in range(16):
                    column = jnp.broadcast_to(tiles[c][8 * part : 8 * part + 8, s : s + 1], (8, 128))
                    if c < 3:
                        column = column - point[c]
                    if c == 2:
                        column = column - height * jnp.floor(column * (1.0 / height) + 0.5)
                    wide[block, c, pl.ds(8 * part, 8), :] = column

    def aim(cy, base, rows):
        face = cells[9, cy, pl.ds(base, 8), :]
        found = [jnp.full((8, 128), FAR, jnp.float32)] * 3 + [jnp.zeros((8, 128), jnp.float32)] * 4
        for q in (-1, 0, 1):
            if not 1 <= cy + q <= 4:
                continue
            for p in (-1, 0, 1):
                if (base < OWN and p != 1) or (base > OWN and p != -1):
                    continue
                hit = face == float(3 * (p + 1) + (q + 1))
                for c in range(7):
                    found[c] = jnp.where(
                        hit, own[c, cy + q - 1, pl.ds(base + p, 8), :], found[c]
                    )
        for c in range(7):
            target[c, cy, pl.ds(base, 8), :] = found[c]

    def aim_own():
        for cy in range(1, 5):
            aim(cy, OWN, None)

    def aim_ring():
        for cy in (0, 5):
            aim(cy, OWN, None)
        for cy in range(6):
            aim(cy, OWN - 8, None)
            aim(cy, OWN + 8, None)

    def wall_block(block, cy, row):
        at = [
            jnp.broadcast_to(target[c, cy, pl.ds(row, 1), :], (8, 128)) for c in range(7)
        ]
        total = [jnp.zeros((8, 128), jnp.float32) for _ in range(3)]
        for part in range(16):
            d = [at[c] - wide[block, c, pl.ds(8 * part, 8), :] for c in range(3)]
            square = d[0] * d[0] + d[1] * d[1] + (d[2] * d[2] + soften)
            inverse = lax.rsqrt(square)
            weight = jnp.maximum(1.0 - square * inverse, 0.0) * inverse
            dot = d[0] * at[3] + d[1] * at[4] + d[2] * at[5]
            repel = at[6] * wide[block, 3, pl.ds(8 * part, 8), :]
            coeff = weight * (repel - weight * dot)
            total = [total[c] + coeff * d[c] for c in range(3)]
        for c in range(3):
            push[c, cy, pl.ds(row, 1), :] = jnp.sum(total[c], axis=0, keepdims=True)

    def walls_rows(low, high):
        def body(b, carry):
            wall_block(b, b // 8, OWN + b % 8)
            return carry

        lax.fori_loop(low, high, body, 0)

    def walls_sides():
        def body(h, carry):
            wall_block(48 + h, h % 6, OWN - 1 + 9 * (h // 6))
            return carry

        lax.fori_loop(0, 12, body, 0)

    def swap(value, step, low):
        return jnp.where(low, pltpu.roll(value, 128 - step, 1), pltpu.roll(value, step, 1))

    low_x = lane % 2 == 0
    low_y = lane // 2 % 2 == 0

    def gather_near(t):
        def body(c, carry):
            comp = jnp.where(c < 6, STATIC + 6 * t + c, jnp.where(c == 6, 0, 1 + t))
            is_x = jnp.where(c == 0, 1.0, 0.0)
            is_y = jnp.where(c == 1, 1.0, 0.0)
            along_x = {-1: [], 0: [], 1: []}
            for cy in range(6):
                mid = cells[comp, cy, pl.ds(OWN, 8), :]
                before = cells[comp, cy, pl.ds(OWN - 1, 8), :]
                after = cells[comp, cy, pl.ds(OWN + 1, 8), :]
                along_x[0].append(mid)
                along_x[1].append(swap(jnp.where(low_x, after, mid), 1, low_x) + is_x)
                along_x[-1].append(swap(jnp.where(low_x, mid, before), 1, low_x) - is_x)
            for p in (-1, 0, 1):
                for cy in range(1, 5):
                    mid, before, after = (along_x[p][cy + q] for q in (0, -1, 1))
                    near[3 * (p + 1) + 1, c, cy - 1] = mid
                    near[3 * (p + 1) + 2, c, cy - 1] = (
                        swap(jnp.where(low_y, after, mid), 2, low_y) + is_y
                    )
                    near[3 * (p + 1), c, cy - 1] = (
                        swap(jnp.where(low_y, mid, before), 2, low_y) - is_y
                    )
            return carry

        lax.fori_loop(0, 8, body, 0)

    def pairs(cy, layer):
        shift = lax.rem(4 * layer + 128, 128)
        back = lax.rem(128 - 4 * layer, 128)
        me = [pltpu.roll(near[4, c, cy], shift, 1) for c in range(8)]
        me[2] = me[2] - layer.astype(jnp.float32) * (1.0 / 3.0)
        total = [jnp.zeros((8, 128), jnp.float32) for _ in range(3)]
        for side in range(9):
            other = [near[side, c, cy] for c in range(8)]
            d = [me[c] - other[c] for c in range(3)]
            square = d[0] * d[0] + d[1] * d[1] + (d[2] * d[2] + soften)
            inverse = lax.rsqrt(square)
            weight = jnp.maximum(1.0 - square * inverse, 0.0) * inverse
            dot = (
                d[0] * (me[3] - other[3]) + d[1] * (me[4] - other[4]) + d[2] * (me[5] - other[5])
            )
            base = me[6] * other[6] + (me[7] + other[7])
            coeff = weight * (base - weight * dot)
            total = [total[c] + coeff * d[c] for c in range(3)]
        return [pltpu.roll(total[c], back, 1) for c in range(3)]

    def all_pairs(reach):
        def cell_body(cy, carry):
            def body(n, total):
                part = pairs(cy, n - 4)
                return tuple(total[c] + part[c] for c in range(3))

            zero = jnp.zeros((8, 128), jnp.float32)
            total = lax.fori_loop(4 - reach, 5 + reach, body, (zero, zero, zero))
            for c in range(3):
                force[c, cy] = total[c]
            return carry

        lax.fori_loop(0, 4, cell_body, 0)

    def collect():
        for cy in range(1, 5):
            total = [force[c, cy - 1] for c in range(3)]
            for p in (-1, 0, 1):
                for q in (-1, 0, 1):
                    rows = pl.ds(OWN - p, 8)
                    hit = cells[9, cy - q, rows, :] == float(3 * (p + 1) + (q + 1))
                    for c in range(3):
                        total[c] = total[c] + jnp.where(hit, push[c, cy - q, rows, :], 0.0)
            for c in range(3):
                force[c, cy - 1] = total[c] * live_ref[cy - 1]

    for t in range(STEPS + 1):
        if t > 0:
            for cy in range(4):
                for c in range(3):
                    half = now[3 + c, cy] + 0.5 * time_step * force[c, cy]
                    now[3 + c, cy] = half
                    now[c, cy] = now[c, cy] + time_step * half
        if t == 0:
            pl.semaphore_wait(barrier, len(greeted))
        copies = publish(t)
        if t == STEPS:
            flags[0] = bad_ref[...]
            row_sent = spread(0, 0, row_of)
        aim_own()
        if t == 0:
            for cy in range(1, 5):
                widen(cy, OWN, range(8), lambda s, cy=cy: 8 * cy + s)
            walls_rows(8, 40)
            for copy in copies:
                copy.wait_recv()
            for cy in (0, 5):
                widen(cy, OWN, range(8), lambda s, cy=cy: 8 * cy + s)
            for cy in range(6):
                widen(cy, OWN - 8, (7,), lambda s, cy=cy: 48 + cy)
                widen(cy, OWN + 8, (0,), lambda s, cy=cy: 54 + cy)
            aim_ring()
            walls_rows(0, 8)
            walls_rows(40, 48)
            walls_sides()
        else:
            aim_ring()
            walls_rows(0, 48)
            walls_sides()
            for copy in copies:
                copy.wait_recv()
        if t == STEPS:
            flags[1] = merged(0, 0, row_sent)
            col_sent = spread(1, tx - 1, col_of)
        gather_near(t)
        all_pairs(3 if t == 0 else 4)
        collect()
        if t == STEPS:
            bad_ref[...] = merged(1, tx - 1, col_sent)
            for copy in row_sent + col_sent:
                copy.wait_send()
        for copy in copies:
            copy.wait_send()
        if t > 0:
            for cy in range(4):
                for c in range(3):
                    now[3 + c, cy] = now[3 + c, cy] + 0.5 * time_step * force[c, cy]

    for cx in range(8):
        for cy in range(4):
            for c in range(3):
                out_x[cx, cy, pl.ds(c, 1), :] = now[c, cy, pl.ds(cx, 1), :]
                out_v[cx, cy, pl.ds(c, 1), :] = now[3 + c, cy, pl.ds(cx, 1), :]


def near_only(positions, velocities, strength, noise, counts, wall_beads, wall_strength, wall_faces):
    vmem = pl.BlockSpec(memory_space=pltpu.VMEM)
    smem = pl.BlockSpec(memory_space=pltpu.SMEM)
    f32 = jnp.float32
    flag_count = lax.axis_size("stream") + lax.axis_size("span") - 2
    return pl.pallas_call(
        kernel,
        out_shape=(
            jax.ShapeDtypeStruct(positions.shape, f32),
            jax.ShapeDtypeStruct(velocities.shape, f32),
            jax.ShapeDtypeStruct((8, 128), f32),
        ),
        in_specs=[smem, smem] + [vmem] * 6,
        out_specs=(vmem, vmem, vmem),
        scratch_shapes=[
            pltpu.VMEM((STATIC + 6 * (STEPS + 1), 6, 24, 128), f32),
            pltpu.VMEM((7, 4, 32, 128), f32),
            pltpu.VMEM((6, 4, 8, 128), f32),
            pltpu.VMEM((4, 8, 128), f32),
            pltpu.VMEM((60, 4, 128, 128), f32),
            pltpu.VMEM((7, 6, 24, 128), f32),
            pltpu.VMEM((3, 6, 24, 128), f32),
            pltpu.VMEM((9, 8, 4, 8, 128), f32),
            pltpu.VMEM((3, 4, 8, 128), f32),
            pltpu.VMEM((2 + flag_count, 8, 128), f32),
            pltpu.SemaphoreType.DMA((STEPS + 1, 8)),
            pltpu.SemaphoreType.DMA((STEPS + 1, 8)),
            pltpu.SemaphoreType.DMA((flag_count,)),
            pltpu.SemaphoreType.DMA((flag_count,)),
        ],
        compiler_params=pltpu.CompilerParams(
            collective_id=0, has_side_effects=True, vmem_limit_bytes=48 * 2**20
        ),
    )(counts, wall_faces, positions, velocities, strength, noise, wall_beads, wall_strength)


def local(*args):
    x, v, bad = near_only(*args)
    worst = jnp.max(bad)
    return lax.cond(worst > 0.0, lambda: every_pair(*args), lambda: (x, v))


def solution(mesh):
    in_specs = (
        P("stream", "span", None, None),
        P("stream", "span", None, None),
        P("stream", "span", None),
        P("stream", "span", None, None),
        P("stream", "span"),
        P("stream", "span", None, None),
        P("stream", "span", None),
        P("stream", "span"),
    )
    out_specs = (P("stream", "span", None, None), P("stream", "span", None, None))
    return jax.shard_map(local, mesh=mesh, in_specs=in_specs, out_specs=out_specs, check_vma=False)
```
